32 devices in a mesh: groups: 2 (over y), tensor: 16 (over z, x, core).
Axes of the slice: x: 2, y: 2, z: 4, core: 2. Of those that a mesh axis runs over, the one named last changes fastest.
Arguments:
- inputs: bfloat16 [256, 14336], P('groups', 'tensor'), parts along dimension 0, may hold values from -6 to 6
- base_weight: bfloat16 [14336, 8192], P('tensor')
- cache_shrink: bfloat16 [8, 16, 14336], P('groups', None, 'tensor'), parts along dimension 0
- cache_expand: bfloat16 [8, 16, 8192], P('groups', None, 'tensor'), parts along dimension 0, may hold values from -0.8984375 to 0.8984375
- cache_magnitude: bfloat16 [8, 8192], P('groups', 'tensor'), parts along dimension 0, may hold values from 0.5 to 2
- store_shrink: bfloat16 [64, 16, 14336], P(('groups', 'tensor')), parts along dimension 0
- store_expand: bfloat16 [64, 16, 8192], P(('groups', 'tensor')), parts along dimension 0, may hold values from -0.8984375 to 0.8984375
- store_magnitude: bfloat16 [64, 8192], P(('groups', 'tensor')), parts along dimension 0, may hold values from 0.5 to 2
- tile_adapter: int32 [16], P('groups'), parts along dimension 0, may hold values from 0 to 31, as said below
- row_adapter: int32 [256], P('groups'), parts along dimension 0, may hold values from 0 to 31, as said below
Outputs:
- adapted: bfloat16 [256, 8192], P('groups', 'tensor'), parts along dimension 0
The draws below stay inside these ranges and needn't reach their ends.
There are 2 independent parts, one for each index of `groups`. The reference program is written for one: setup_inputs(seed, part) draws one part's arguments, and reference() takes and returns one part's arrays. A program takes and returns all parts, laid end to end along the dimension named above; an argument that names none is the same for every part. Nothing has to cross between parts.
Inputs may be any that keep to these rules, and one draw needn't show every extreme that they name: `tile_adapter`: 8 different adapter ids; adapters 2j and 2j + 1 are the entries of store_shrink, store_expand and store_magnitude held by tensor index j; the last 4 ids lie on 4 different tensor indices, so no index holds more than one of them. `row_adapter`: every row's id is one of tile_adapter's, and every tile has at least one row.
All inputs are finite; a program needn't handle non-finite values.
Results may differ from the reference program's by a relative error of at most 0.0004.
Values may be sent and summed in bfloat16 or wider, within the bound.
A program may use at most 128 MiB of HBM per device.

```python
import math
import jax
import jax.numpy as jnp
from jax import lax

D = 8192
FF = 14336
R = 16
ROWS = 128
RESIDENT = 4
NEW = 4
TILES = 8
ADAPTERS = 32
N_TENSOR = 16


def tile_ids(key):
    devices = jax.random.permutation(jax.random.fold_in(key, 11), N_TENSOR)
    halves = jax.random.randint(jax.random.fold_in(key, 12), (RESIDENT + NEW,), 0, 2)
    return (2 * devices[:RESIDENT + NEW] + halves).astype(jnp.int32)


def draw_tile_adapter(key, part):
    return tile_ids(key)


def draw_row_adapter(key, part):
    tiles = tile_ids(key)
    key = jax.random.fold_in(key, 3)
    first = jax.random.permutation(jax.random.fold_in(key, 1), TILES)
    others = jax.random.randint(jax.random.fold_in(key, 2), (ROWS - TILES,), 0, TILES)
    order = jax.random.permutation(jax.random.fold_in(key, 4), ROWS)
    picks = jnp.concatenate([first, others]).astype(jnp.int32)[order]
    return tiles[picks]


def draw_base_weight(key, part):
    key = jax.random.fold_in(key, 5)
    key_vals, key_rows, key_cols, key_signs = jax.random.split(key, 4)
    ramp = jnp.power(3.0, jnp.arange(FF, dtype=jnp.float32) / FF)
    row_scale = jnp.exp(jax.random.uniform(key_rows, (FF, 1)) * math.log(10.0)) * ramp[:, None]
    col_signs = (2 * jax.random.randint(key_signs, (1, D), 0, 2) - 1).astype(jnp.float32)
    values = jax.random.normal(key_vals, (FF, D))
    col_scale = jnp.exp(jax.random.uniform(key_cols, (1, D)) * math.log(10.0))
    values = values + 0.45 * col_signs
    return (values * row_scale * col_scale / math.sqrt(78.0 * FF)).astype(jnp.bfloat16)


def shrink_rows(key, noise, count):
    key_sign, key_size = jax.random.split(key, 2)
    signs = (2 * jax.random.randint(key_sign, (count, R, 1), 0, 2) - 1).astype(jnp.float32)
    sizes = jax.random.uniform(key_size, (count, R, 1), minval=0.6, maxval=1.4)
    return ((noise + signs * sizes) / math.sqrt(FF)).astype(jnp.bfloat16)


def draw_cache_shrink(key, part):
    key = jax.random.fold_in(key, 21)
    key_noise, key_rows = jax.random.split(key, 2)
    noise = jax.random.normal(key_noise, (RESIDENT, R, FF))
    return shrink_rows(key_rows, noise, RESIDENT)


def draw_store_shrink(key, part):
    key = jax.random.fold_in(key, 22)
    key_noise, key_rows = jax.random.split(key, 2)
    noise = jax.random.normal(key_noise, (ADAPTERS, R, FF))
    return shrink_rows(key_rows, noise, ADAPTERS)


def block_scale(key, extent, pieces, smallest, high):
    level = 1.0
    for dim, blocks in pieces:
        steps = jax.random.uniform(jax.random.fold_in(jax.random.fold_in(key, 6), dim), (blocks,), jnp.float32, smallest / len(pieces), high / len(pieces))
        level = level * jnp.repeat(jnp.exp(steps), extent[dim] // blocks).reshape((-1,) + (1,) * (len(extent) - 1 - dim))
    return level


def bell_draw(own_key, dims, width, limit, shards=(), held_as=jnp.bfloat16):
    values = jax.random.normal(own_key, dims, jnp.float32) * width
    if len(shards) > 0:
        values = block_scale(own_key, dims, shards, -0.22, 0.18) * values
    return jnp.clip(values, min=-limit, max=limit).astype(held_as)


def setup_inputs(seed: int = 0, part: int = 0) -> dict:
    streams_of = jax.random.split(jax.random.key(seed), 11)
    part_splits = jax.random.split(jax.random.fold_in(streams_of[10], part), 11)
    inputs = bell_draw(part_splits[0], (ROWS, FF), 1.0, 6.0, ((1, 16),))
    base_weight = draw_base_weight(jax.random.fold_in(streams_of[10], 71), part)
    cache_shrink = draw_cache_shrink(jax.random.fold_in(jax.random.fold_in(streams_of[10], part), 71), part)
    cache_expand = bell_draw(part_splits[3], (RESIDENT, R, D), 0.15, 0.8984375, ((2, 16),))
    cache_magnitude = jnp.clip(jnp.exp(math.log(2.0) - 1.3862944 * jax.random.uniform(part_splits[4], (RESIDENT, D), jnp.float32) ** block_scale(part_splits[4], (RESIDENT, D), ((1, 16),), -0.2, 0.2)), 0.5, 2.0).astype(jnp.bfloat16)
    store_shrink = draw_store_shrink(jax.random.fold_in(jax.random.fold_in(streams_of[10], part), 71), part)
    store_expand = bell_draw(part_splits[6], (ADAPTERS, R, D), 0.15, 0.8984375, ((0, 16),))
    store_magnitude = jnp.clip(jnp.exp(math.log(2.0) - 1.3862944 * jax.random.uniform(part_splits[7], (ADAPTERS, D), jnp.float32) ** block_scale(part_splits[7], (ADAPTERS, D), ((0, 16),), -0.2, 0.2)), 0.5, 2.0).astype(jnp.bfloat16)
    tile_adapter = draw_tile_adapter(jax.random.fold_in(jax.random.fold_in(streams_of[10], part), 71), part)
    row_adapter = draw_row_adapter(jax.random.fold_in(jax.random.fold_in(streams_of[10], part), 71), part)
    return {"inputs": inputs, "base_weight": base_weight, "cache_shrink": cache_shrink, "cache_expand": cache_expand, "cache_magnitude": cache_magnitude, "store_shrink": store_shrink, "store_expand": store_expand, "store_magnitude": store_magnitude, "tile_adapter": tile_adapter, "row_adapter": row_adapter}


ADAPTER_SCALING = 2.0

def reference(inputs, base_weight, cache_shrink, cache_expand, cache_magnitude, store_shrink, store_expand, store_magnitude, tile_adapter, row_adapter):
    highest_precision = lax.Precision.HIGHEST
    new_ids = tile_adapter[RESIDENT:]
    down_factor = jnp.concatenate([cache_shrink, store_shrink[new_ids]], 0).astype(jnp.float32)
    expand = jnp.concatenate([cache_expand, store_expand[new_ids]], 0).astype(jnp.float32)
    magnitude = jnp.concatenate([cache_magnitude, store_magnitude[new_ids]], 0).astype(jnp.float32)
    weight = base_weight.astype(jnp.float32)
    flat_shrink = down_factor.reshape(TILES * R, FF)
    row_tile = (row_adapter[:, None] == tile_adapter[None, :]).astype(jnp.float32)
    activ = inputs.astype(jnp.float32)
    projected = jnp.dot(activ, flat_shrink.T, precision=highest_precision)
    low = jnp.einsum('kt,ktr->kr', row_tile, projected.reshape(ROWS, TILES, R), precision=highest_precision)
    frozen_output = jnp.dot(activ, weight, precision=highest_precision)
    column_square_sums = lax.optimization_barrier(jnp.sum(weight * weight, axis=0))
    cross = jnp.dot(weight.T, flat_shrink.T, precision=highest_precision).reshape(D, TILES, R)
    partial_gram_matrix = jnp.einsum('aig,ahg->aih', down_factor, down_factor, precision=highest_precision)
    linear_term = jnp.einsum('dtr,trd->td', cross, expand, precision=highest_precision)
    quadratic_term = lax.optimization_barrier(jnp.sum(expand * jnp.einsum('trq,tqd->trd', partial_gram_matrix, expand, precision=highest_precision), axis=1))
    squared_norm = column_square_sums[None, :] + 2.0 * ADAPTER_SCALING * linear_term + ADAPTER_SCALING * ADAPTER_SCALING * quadratic_term
    factor = magnitude / jnp.sqrt(squared_norm)
    spread = (row_tile[:, :, None] * low[:, None, :]).reshape(ROWS, TILES * R)
    low_rank_update = jnp.dot(spread, expand.reshape(TILES * R, D), precision=highest_precision)
    row_multiplier = jnp.dot(row_tile, factor, precision=highest_precision)
    return (row_multiplier * (frozen_output + ADAPTER_SCALING * low_rank_update)).astype(jnp.bfloat16)
```

```python
import functools

import jax
import jax.numpy as jnp
from jax import lax
from jax.experimental import pallas as pl
from jax.experimental.pallas import tpu as pltpu
from jax.sharding import PartitionSpec as P

ADAPTER_SCALING = 2.0


def plain_local(
    inputs,
    base_weight,
    cache_shrink,
    cache_expand,
    cache_magnitude,
    store_shrink,
    store_expand,
    store_magnitude,
    tile_adapter,
    row_adapter,
):
    highest_precision = lax.Precision.HIGHEST
    position = lax.axis_index("tensor")
    slot_count = store_shrink.shape[0]
    resident = cache_shrink.shape[0]
    new_ids = tile_adapter[resident:]
    owners = new_ids // slot_count
    owned = owners == position
    chosen = jnp.sum(jnp.where(owned, new_ids % slot_count, 0))
    present = jnp.any(owned)

    def select_piece(stored):
        segment = lax.dynamic_index_in_dim(stored, chosen, 0, keepdims=True)
        return jnp.where(present, segment, jnp.zeros_like(segment))

    sent_shrink = select_piece(store_shrink)
    sent_expand = select_piece(store_expand)
    sent_magnitude = select_piece(store_magnitude)[:, None, :]
    got_shrink, got_expand, got_magnitude = (
        lax.all_to_all(sent_shrink, "tensor", split_axis=2, concat_axis=0, tiled=True),
        lax.all_to_all(sent_expand, "tensor", split_axis=2, concat_axis=0, tiled=True),
        lax.all_to_all(sent_magnitude, "tensor", split_axis=2, concat_axis=0, tiled=True),
    )
    down_factor = jnp.concatenate([cache_shrink, jnp.take(got_shrink, owners, axis=0)], 0)
    expand = jnp.concatenate([cache_expand, jnp.take(got_expand, owners, axis=0)], 0)
    magnitude = jnp.concatenate(
        [cache_magnitude, jnp.take(got_magnitude, owners, axis=0)[:, 0, :]], 0
    ).astype(jnp.float32)
    tile_count = down_factor.shape[0]
    rank_size = down_factor.shape[1]
    row_count = inputs.shape[0]
    own_width = expand.shape[2]
    flat_shrink = down_factor.reshape(tile_count * rank_size, down_factor.shape[2])
    row_tile = (row_adapter[:, None] == tile_adapter[None, :]).astype(jnp.float32)
    projected = lax.dot_general(
        inputs, flat_shrink, (((1,), (1,)), ((), ())), preferred_element_type=jnp.float32
    )
    low_part = jnp.sum(
        row_tile[:, :, None] * projected.reshape(row_count, tile_count, rank_size), axis=1
    )
    base_part = jnp.dot(inputs, base_weight, preferred_element_type=jnp.float32)
    expand_wide = expand.astype(jnp.float32)
    col_part = jnp.sum(jnp.square(base_weight.astype(jnp.float32)), axis=0)
    partial_gram_matrix = jnp.einsum(
        "aig,ahg->aih", down_factor, down_factor, preferred_element_type=jnp.float32
    )
    low, gram_sum, column_square_sums = lax.psum(
        (low_part, partial_gram_matrix, col_part), "tensor"
    )
    cross = lax.psum_scatter(
        lax.dot_general(
            base_weight, flat_shrink, (((0,), (1,)), ((), ())), preferred_element_type=jnp.float32
        ),
        "tensor",
        scatter_dimension=0,
        tiled=True,
    ).reshape(own_width, tile_count, rank_size)
    frozen_output = lax.psum_scatter(base_part, "tensor", scatter_dimension=1, tiled=True)
    local_column_slice = lax.dynamic_slice_in_dim(
        column_square_sums, position * own_width, own_width
    )
    linear_term = jnp.einsum("dtr,trd->td", cross, expand_wide, precision=highest_precision)
    quadratic_term = jnp.sum(
        expand_wide
        * jnp.einsum("trq,tqd->trd", gram_sum, expand_wide, precision=highest_precision),
        axis=1,
    )
    squared_norm = (
        local_column_slice[None, :]
        + 2.0 * ADAPTER_SCALING * linear_term
        + ADAPTER_SCALING * ADAPTER_SCALING * quadratic_term
    )
    factor = magnitude / jnp.sqrt(squared_norm)
    spread = (row_tile[:, :, None] * low[:, None, :]).reshape(row_count, tile_count * rank_size)
    low_rank_update = jnp.dot(
        spread, expand_wide.reshape(tile_count * rank_size, own_width), precision=highest_precision
    )
    row_multiplier = jnp.dot(row_tile, factor, precision=highest_precision)
    return (row_multiplier * (frozen_output + ADAPTER_SCALING * low_rank_update)).astype(
        jnp.bfloat16
    )


LAG = 4
MESH = pl.DeviceIdType.MESH


def split3(value):
    high = value.astype(jnp.bfloat16)
    rest = value - high.astype(jnp.float32)
    middle = rest.astype(jnp.bfloat16)
    low = (rest - middle.astype(jnp.float32)).astype(jnp.bfloat16)
    return high, middle, low


def exact_dot(left, right, dims):
    return sum(
        lax.dot_general(part, right, (dims, ((), ())), preferred_element_type=jnp.float32)
        for part in reversed(split3(left))
    )


def fused_kernel(
    n,
    owners_ref,
    inputs_ref,
    weight_ref,
    cache_shrink_ref,
    cache_expand_ref,
    cache_magnitude_ref,
    shrink_ref,
    expand_ref,
    magnitude_ref,
    row_mask_ref,
    out_ref,
    weight_buf,
    got_shrink,
    got_expand,
    got_magnitude,
    flat_shrink,
    flat_expand,
    base_pair_out,
    base_pair_in,
    base_ring_out,
    base_ring_in,
    cross_pair_out,
    cross_pair_in,
    cross_ring_out,
    cross_ring_in,
    base_sum,
    cross_sum,
    small_out,
    small_in,
    weight_sem,
    piece_send,
    piece_recv,
    pair_send,
    pair_recv,
    ring_send,
    ring_recv,
    small_send,
    small_recv,
):
    me = lax.axis_index("tensor")
    chips = n // 2
    half = n // 4
    core = lax.rem(me, 2)
    chip = lax.div(me, 2)
    across = lax.rem(chip, 2)
    along = lax.div(chip, 2)
    place = along + across * (2 * half - 1 - 2 * along)
    step = 1 - 2 * core

    def device_at(spot, which):
        spot = lax.rem(spot + 4 * chips, chips)
        side = lax.div(spot, half)
        depth = spot + side * (2 * half - 1 - 2 * spot)
        return (depth * 2 + side) * 2 + which

    partner = device_at(place, 1 - core)
    following = device_at(place + step, core)
    rows, hidden = inputs_ref.shape
    width = out_ref.shape[1]
    rank = shrink_ref.shape[0]
    new = owners_ref.shape[0]
    resident_rows = cache_shrink_ref.shape[0]
    tile_rows = flat_shrink.shape[0]
    tiles = tile_rows // rank

    def weight_copy(slot):
        turn = lax.div(slot, 2)
        own = lax.rem(slot, 2)
        spot = place + (1 - 2 * own) * step * (1 + turn)
        which = own * core + (1 - own) * (1 - core)
        block = device_at(spot, which)
        column = pl.multiple_of(block * width, width)
        return pltpu.make_async_copy(
            weight_ref.at[:, pl.ds(column, width)], weight_buf.at[slot], weight_sem.at[slot]
        )

    def start_weight(slot, carry):
        weight_copy(slot).start()
        return carry

    lax.fori_loop(0, n, start_weight, 0)

    barrier = pltpu.get_barrier_semaphore()

    def greet(offset, carry):
        pl.semaphore_signal(
            barrier,
            inc=1,
            device_id={"tensor": lax.rem(me + offset, n)},
            device_id_type=MESH,
        )
        return carry

    lax.fori_loop(1, n, greet, 0)
    pl.semaphore_wait(barrier, n - 1)

    def piece_parts(target):
        shrink_column = pl.multiple_of(target * hidden, 128)
        expand_column = pl.multiple_of(target * width, 128)
        return (
            (shrink_ref.at[:, pl.ds(shrink_column, hidden)], got_shrink),
            (expand_ref.at[:, pl.ds(expand_column, width)], got_expand),
            (magnitude_ref.at[target], got_magnitude),
        )

    def piece_copies(offset):
        target = lax.rem(me + offset, n)
        return [
            pltpu.make_async_remote_copy(
                src_ref=source,
                dst_ref=landing.at[me],
                send_sem=piece_send.at[kind, offset],
                recv_sem=piece_recv.at[kind, me],
                device_id={"tensor": target},
                device_id_type=MESH,
            )
            for kind, (source, landing) in enumerate(piece_parts(target))
        ]

    def start_pieces(offset, carry):
        for copy in piece_copies(offset):
            copy.start()
        return carry

    def piece_sent(offset, carry):
        for copy in piece_copies(offset):
            copy.wait_send()
        return carry

    def own_pieces():
        return [
            pltpu.make_async_copy(source, landing.at[me], piece_recv.at[kind, me])
            for kind, (source, landing) in enumerate(piece_parts(me))
        ]

    def piece_arrived(sender, carry):
        for kind, landing in enumerate((got_shrink, got_expand, got_magnitude)):
            pltpu.make_async_copy(
                landing.at[sender], landing.at[sender], piece_recv.at[kind, sender]
            ).wait()
        return carry

    def pair_copy(chain, turn):
        source, landing = ((base_pair_out, base_pair_in), (cross_pair_out, cross_pair_in))[chain]
        return pltpu.make_async_remote_copy(
            src_ref=source.at[turn],
            dst_ref=landing.at[turn],
            send_sem=pair_send.at[chain, turn],
            recv_sem=pair_recv.at[chain, turn],
            device_id={"tensor": partner},
            device_id_type=MESH,
        )

    def ring_copy(chain, turn):
        source, landing = ((base_ring_out, base_ring_in), (cross_ring_out, cross_ring_in))[chain]
        return pltpu.make_async_remote_copy(
            src_ref=source.at[turn],
            dst_ref=landing.at[turn],
            send_sem=ring_send.at[chain, turn],
            recv_sem=ring_recv.at[chain, turn],
            device_id={"tensor": following},
            device_id_type=MESH,
        )

    def small_copy(offset):
        return pltpu.make_async_remote_copy(
            src_ref=small_out,
            dst_ref=small_in.at[me],
            send_sem=small_send.at[offset],
            recv_sem=small_recv.at[me],
            device_id={"tensor": lax.rem(me + offset, n)},
            device_id_type=MESH,
        )

    def squares(slot):
        chunk = 64

        def add(index, total):
            part = weight_buf[slot, pl.ds(pl.multiple_of(index * chunk, chunk), chunk), :]
            part = part.astype(jnp.float32)
            return total + jnp.sum((part * part).reshape(chunk // 8, 8, width), axis=0)

        return lax.fori_loop(0, hidden // chunk, add, jnp.zeros((8, width), jnp.float32))

    def product(chain, slot):
        left = (inputs_ref, flat_shrink)[chain]
        return jnp.dot(left[...], weight_buf[slot], preferred_element_type=jnp.float32)

    def to_partner(chain, turn):
        slot = 2 * turn
        out = (base_pair_out, cross_pair_out)[chain]
        if chain == 0:
            weight_copy(slot).wait()
            out[turn, pl.ds(rows, 8), :] = squares(slot)
        out[turn, pl.ds(0, rows if chain == 0 else tile_rows), :] = product(chain, slot)
        pair_copy(chain, turn).start()

    def ring_turn(chain, turn):
        slot = 2 * turn + 1
        total = (base_sum, cross_sum)[chain]
        ring_out = (base_ring_out, cross_ring_out)[chain]
        ring_in = (base_ring_in, cross_ring_in)[chain]
        pair_in = (base_pair_in, cross_pair_in)[chain]
        if chain == 0:
            weight_copy(slot).wait()
            total[pl.ds(rows, 8), :] = squares(slot)
        total[pl.ds(0, rows if chain == 0 else tile_rows), :] = product(chain, slot)
        pair_copy(chain, turn).wait_recv()
        total[...] += pair_in[turn]

        @pl.when(turn > 0)
        def _():
            ring_copy(chain, turn - 1).wait_recv()
            total[...] += ring_in[turn - 1]

        @pl.when(turn < chips - 1)
        def _():
            ring_out[turn] = total[...]
            ring_copy(chain, turn).start()

    def adapters_ready():
        lax.fori_loop(0, n, piece_arrived, 0)
        flat_shrink[pl.ds(0, resident_rows), :] = cache_shrink_ref[...]
        flat_expand[pl.ds(0, resident_rows), :] = cache_expand_ref[...]
        for tile in range(new):
            owner = owners_ref[tile]
            target = pl.ds(resident_rows + tile * rank, rank)
            flat_shrink[target, :] = got_shrink[owner]
            flat_expand[target, :] = got_expand[owner]
        shrink = flat_shrink[...]
        contract = (((1,), (1,)), ((), ()))
        low = lax.dot_general(
            shrink, inputs_ref[...], contract, preferred_element_type=jnp.float32
        )
        gram = lax.dot_general(shrink, shrink, contract, preferred_element_type=jnp.float32)
        low = jnp.sum((low * row_mask_ref[...]).reshape(tiles, rank, rows), axis=0)
        gram = jnp.where(tile_mask(), gram, 0.0)
        gram = jnp.sum(gram.reshape(tiles, rank, tile_rows), axis=0)
        small_out[pl.ds(0, rank), :] = low
        small_out[pl.ds(rank, rank), :] = gram

        def send(offset, carry):
            small_copy(offset).start()
            return carry

        lax.fori_loop(1, n, send, 0)

    def tile_mask():
        shape = (tile_rows, tile_rows)
        first = lax.broadcasted_iota(jnp.int32, shape, 0) // rank
        second = lax.broadcasted_iota(jnp.int32, shape, 1) // rank
        return first == second

    to_partner(0, 0)
    for copy in own_pieces():
        copy.start()
    lax.fori_loop(1, n, start_pieces, 0)

    def turn_body(turn, carry):
        @pl.when(turn < chips - 1)
        def _():
            to_partner(0, turn + 1)

        @pl.when(turn < chips)
        def _():
            ring_turn(0, turn)

        @pl.when(turn == LAG - 1)
        def _():
            adapters_ready()
            to_partner(1, 0)

        @pl.when((turn >= LAG) & (turn < chips + LAG - 1))
        def _():
            to_partner(1, turn - LAG + 1)

        @pl.when(turn >= LAG)
        def _():
            ring_turn(1, turn - LAG)

        return carry

    lax.fori_loop(0, chips + LAG, turn_body, 0)

    def add_small(offset, total):
        sender = lax.rem(me + offset, n)
        pltpu.make_async_copy(
            small_in.at[sender], small_in.at[sender], small_recv.at[sender]
        ).wait()
        return total + small_in[sender]

    small = lax.fori_loop(1, n, add_small, small_out[...])
    low = jnp.concatenate([small[:rank]] * tiles, 0)
    gram = jnp.where(tile_mask(), jnp.concatenate([small[rank:]] * tiles, 0), 0.0)
    expand = flat_expand[...]
    wide = expand.astype(jnp.float32)
    quadratic = exact_dot(gram, expand, ((1,), (0,)))
    change = jnp.sum(
        (wide * (cross_sum[...] + quadratic)).reshape(tiles, rank, width), axis=1
    )
    column_squares = jnp.sum(base_sum[pl.ds(rows, 8), :], axis=0, keepdims=True)
    squared_norm = column_squares + 2.0 * ADAPTER_SCALING * change
    magnitude = jnp.concatenate(
        [cache_magnitude_ref[...]] + [got_magnitude[owners_ref[t]] for t in range(new)], 0
    )
    factor = magnitude / jnp.sqrt(squared_norm)
    row_mask = row_mask_ref[...]
    update = exact_dot(low * row_mask, expand, ((0,), (0,)))
    spread = jnp.broadcast_to(factor[:, None, :], (tiles, rank, width)).reshape(tile_rows, width)
    pick = lax.broadcasted_iota(jnp.int32, row_mask.shape, 0) % rank == 0
    pick = jnp.where(pick, row_mask, 0.0).astype(jnp.bfloat16)
    multiplier = sum(
        lax.dot_general(
            pick, part, (((0,), (0,)), ((), ())), preferred_element_type=jnp.float32
        )
        for part in reversed(split3(spread))
    )
    base = base_sum[pl.ds(0, rows), :]
    out_ref[...] = (multiplier * (base + ADAPTER_SCALING * update)).astype(out_ref.dtype)

    lax.fori_loop(1, n, piece_sent, 0)

    def small_sent(offset, carry):
        small_copy(offset).wait_send()
        return carry

    lax.fori_loop(1, n, small_sent, 0)

    def turn_sent(turn, carry):
        for chain in range(2):
            pair_copy(chain, turn).wait_send()

            @pl.when(turn < chips - 1)
            def _():
                ring_copy(chain, turn).wait_send()

        return carry

    lax.fori_loop(0, chips, turn_sent, 0)


def fused_local(
    n,
    inputs,
    base_weight,
    cache_shrink,
    cache_expand,
    cache_magnitude,
    store_shrink,
    store_expand,
    store_magnitude,
    tile_adapter,
    row_adapter,
):
    position = lax.axis_index("tensor")
    slot_count, rank, _ = store_shrink.shape
    resident, _, hidden = cache_shrink.shape
    width = cache_expand.shape[2]
    rows = inputs.shape[0]
    tiles = tile_adapter.shape[0]
    tile_rows = tiles * rank
    owners = tile_adapter[resident:] // slot_count
    chosen = jnp.sum(
        jnp.where(owners == position, tile_adapter[resident:] % slot_count, 0)
    )

    def select(stored):
        return lax.dynamic_index_in_dim(stored, chosen, 0, keepdims=False)

    row_mask = (jnp.repeat(tile_adapter, rank)[:, None] == row_adapter[None, :]).astype(
        jnp.float32
    )
    chips = n // 2
    tall = rows + 8
    vmem = pl.BlockSpec(memory_space=pltpu.VMEM)
    return pl.pallas_call(
        functools.partial(fused_kernel, n),
        out_shape=jax.ShapeDtypeStruct((rows, width), jnp.bfloat16),
        in_specs=[pl.BlockSpec(memory_space=pltpu.SMEM), vmem, pl.BlockSpec(memory_space=pl.ANY)]
        + [vmem] * 7,
        out_specs=vmem,
        scratch_shapes=[
            pltpu.VMEM((n, hidden, width), jnp.bfloat16),
            pltpu.VMEM((n, rank, hidden), jnp.bfloat16),
            pltpu.VMEM((n, rank, width), jnp.bfloat16),
            pltpu.VMEM((n, 1, width), jnp.float32),
            pltpu.VMEM((tile_rows, hidden), jnp.bfloat16),
            pltpu.VMEM((tile_rows, width), jnp.bfloat16),
            pltpu.VMEM((chips, tall, width), jnp.float32),
            pltpu.VMEM((chips, tall, width), jnp.float32),
            pltpu.VMEM((chips - 1, tall, width), jnp.float32),
            pltpu.VMEM((chips - 1, tall, width), jnp.float32),
            pltpu.VMEM((chips, tile_rows, width), jnp.float32),
            pltpu.VMEM((chips, tile_rows, width), jnp.float32),
            pltpu.VMEM((chips - 1, tile_rows, width), jnp.float32),
            pltpu.VMEM((chips - 1, tile_rows, width), jnp.float32),
            pltpu.VMEM((tall, width), jnp.float32),
            pltpu.VMEM((tile_rows, width), jnp.float32),
            pltpu.VMEM((2 * rank, rows), jnp.float32),
            pltpu.VMEM((n, 2 * rank, rows), jnp.float32),
            pltpu.SemaphoreType.DMA((n,)),
            pltpu.SemaphoreType.DMA((3, n)),
            pltpu.SemaphoreType.DMA((3, n)),
            pltpu.SemaphoreType.DMA((2, chips)),
            pltpu.SemaphoreType.DMA((2, chips)),
            pltpu.SemaphoreType.DMA((2, chips)),
            pltpu.SemaphoreType.DMA((2, chips)),
            pltpu.SemaphoreType.DMA((n,)),
            pltpu.SemaphoreType.DMA((n,)),
        ],
        compiler_params=pltpu.CompilerParams(
            collective_id=0, has_side_effects=True, vmem_limit_bytes=56 * 1024 * 1024
        ),
    )(
        owners,
        inputs,
        base_weight,
        cache_shrink.reshape(resident * rank, hidden),
        cache_expand.reshape(resident * rank, width),
        cache_magnitude.astype(jnp.float32),
        select(store_shrink),
        select(store_expand),
        select(store_magnitude).astype(jnp.float32).reshape(n, 1, width),
        row_mask,
    )


def fits_kernel(n, inputs, cache_shrink, cache_expand, tile_adapter):
    rank = cache_shrink.shape[1]
    rows = inputs.shape[0]
    tile_rows = tile_adapter.shape[0] * rank
    return (
        n % 4 == 0
        and cache_shrink.shape[2] % 128 == 0
        and cache_expand.shape[2] % 128 == 0
        and rank % 16 == 0
        and rows == tile_rows
        and rows % 128 == 0
        and n * cache_shrink.shape[2] * cache_expand.shape[2] <= 2**23
    )


def local(n, *args):
    if fits_kernel(n, args[0], args[2], args[3], args[8]):
        return fused_local(n, *args)
    return plain_local(*args)


def solution(mesh):
    in_specs = (
        P("groups", "tensor"),
        P("tensor", None),
        P("groups", None, "tensor"),
        P("groups", None, "tensor"),
        P("groups", "tensor"),
        P(("groups", "tensor"), None, None),
        P(("groups", "tensor"), None, None),
        P(("groups", "tensor"), None),
        P("groups"),
        P("groups"),
    )
    out_specs = P("groups", "tensor")
    body = functools.partial(local, mesh.shape["tensor"])
    return jax.shard_map(body, mesh=mesh, in_specs=in_specs, out_specs=out_specs, check_vma=False)
```

```python
import functools

import jax
import jax.numpy as jnp
from jax import lax
from jax.experimental import pallas as pl
from jax.experimental.pallas import tpu as pltpu
from jax.sharding import PartitionSpec as P

ADAPTER_SCALING = 2.0


def plain_local(
    inputs,
    base_weight,
    cache_shrink,
    cache_expand,
    cache_magnitude,
    store_shrink,
    store_expand,
    store_magnitude,
    tile_adapter,
    row_adapter,
):
    highest_precision = lax.Precision.HIGHEST
    position = lax.axis_index("tensor")
    slot_count = store_shrink.shape[0]
    resident = cache_shrink.shape[0]
    new_ids = tile_adapter[resident:]
    owners = new_ids // slot_count
    owned = owners == position
    chosen = jnp.sum(jnp.where(owned, new_ids % slot_count, 0))
    present = jnp.any(owned)

    def select_piece(stored):
        segment = lax.dynamic_index_in_dim(stored, chosen, 0, keepdims=True)
        return jnp.where(present, segment, jnp.zeros_like(segment))

    sent_shrink = select_piece(store_shrink)
    sent_expand = select_piece(store_expand)
    sent_magnitude = select_piece(store_magnitude)[:, None, :]
    got_shrink, got_expand, got_magnitude = (
        lax.all_to_all(sent_shrink, "tensor", split_axis=2, concat_axis=0, tiled=True),
        lax.all_to_all(sent_expand, "tensor", split_axis=2, concat_axis=0, tiled=True),
        lax.all_to_all(sent_magnitude, "tensor", split_axis=2, concat_axis=0, tiled=True),
    )
    down_factor = jnp.concatenate([cache_shrink, jnp.take(got_shrink, owners, axis=0)], 0)
    expand = jnp.concatenate([cache_expand, jnp.take(got_expand, owners, axis=0)], 0)
    magnitude = jnp.concatenate(
        [cache_magnitude, jnp.take(got_magnitude, owners, axis=0)[:, 0, :]], 0
    ).astype(jnp.float32)
    tile_count = down_factor.shape[0]
    rank_size = down_factor.shape[1]
    row_count = inputs.shape[0]
    own_width = expand.shape[2]
    flat_shrink = down_factor.reshape(tile_count * rank_size, down_factor.shape[2])
    row_tile = (row_adapter[:, None] == tile_adapter[None, :]).astype(jnp.float32)
    projected = lax.dot_general(
        inputs, flat_shrink, (((1,), (1,)), ((), ())), preferred_element_type=jnp.float32
    )
    low_part = jnp.sum(
        row_tile[:, :, None] * projected.reshape(row_count, tile_count, rank_size), axis=1
    )
    base_part = jnp.dot(inputs, base_weight, preferred_element_type=jnp.float32)
    expand_wide = expand.astype(jnp.float32)
    col_part = jnp.sum(jnp.square(base_weight.astype(jnp.float32)), axis=0)
    partial_gram_matrix = jnp.einsum(
        "aig,ahg->aih", down_factor, down_factor, preferred_element_type=jnp.float32
    )
    low, gram_sum, column_square_sums = lax.psum(
        (low_part, partial_gram_matrix, col_part), "tensor"
    )
    cross = lax.psum_scatter(
        lax.dot_general(
            base_weight, flat_shrink, (((0,), (1,)), ((), ())), preferred_element_type=jnp.float32
        ),
        "tensor",
        scatter_dimension=0,
        tiled=True,
    ).reshape(own_width, tile_count, rank_size)
    frozen_output = lax.psum_scatter(base_part, "tensor", scatter_dimension=1, tiled=True)
    local_column_slice = lax.dynamic_slice_in_dim(
        column_square_sums, position * own_width, own_width
    )
    linear_term = jnp.einsum("dtr,trd->td", cross, expand_wide, precision=highest_precision)
    quadratic_term = jnp.sum(
        expand_wide
        * jnp.einsum("trq,tqd->trd", gram_sum, expand_wide, precision=highest_precision),
        axis=1,
    )
    squared_norm = (
        local_column_slice[None, :]
        + 2.0 * ADAPTER_SCALING * linear_term
        + ADAPTER_SCALING * ADAPTER_SCALING * quadratic_term
    )
    factor = magnitude / jnp.sqrt(squared_norm)
    spread = (row_tile[:, :, None] * low[:, None, :]).reshape(row_count, tile_count * rank_size)
    low_rank_update = jnp.dot(
        spread, expand_wide.reshape(tile_count * rank_size, own_width), precision=highest_precision
    )
    row_multiplier = jnp.dot(row_tile, factor, precision=highest_precision)
    return (row_multiplier * (frozen_output + ADAPTER_SCALING * low_rank_update)).astype(
        jnp.bfloat16
    )


LAG = 3
PARTS = 2
MESH = pl.DeviceIdType.MESH


def split3(value):
    high = value.astype(jnp.bfloat16)
    rest = value - high.astype(jnp.float32)
    middle = rest.astype(jnp.bfloat16)
    low = (rest - middle.astype(jnp.float32)).astype(jnp.bfloat16)
    return high, middle, low


def exact_dot(left, right, dims):
    return sum(
        lax.dot_general(part, right, (dims, ((), ())), preferred_element_type=jnp.float32)
        for part in reversed(split3(left))
    )


def fused_kernel(
    n,
    tiles_ref,
    inputs_ref,
    weight_ref,
    cache_shrink_ref,
    cache_expand_ref,
    cache_magnitude_ref,
    store_shrink_ref,
    store_expand_ref,
    store_magnitude_ref,
    row_adapter_ref,
    out_ref,
    weight_buf,
    store_shrink_buf,
    store_expand_buf,
    shrink_ref,
    expand_ref,
    magnitude_ref,
    row_mask_ref,
    got_shrink,
    got_expand,
    got_magnitude,
    flat_shrink,
    flat_expand,
    base_pair_out,
    base_pair_in,
    base_ring_out,
    base_ring_in,
    cross_pair_out,
    cross_pair_in,
    cross_ring_out,
    cross_ring_in,
    small_out,
    small_in,
    weight_sem,
    store_sem,
    piece_send,
    piece_recv,
    pair_send,
    pair_recv,
    ring_send,
    ring_recv,
    small_send,
    small_recv,
):
    me = lax.axis_index("tensor")
    chips = n // 2
    half = n // 4
    core = lax.rem(me, 2)
    chip = lax.div(me, 2)
    across = lax.rem(chip, 2)
    along = lax.div(chip, 2)
    place = along + across * (2 * half - 1 - 2 * along)
    step = 1 - 2 * core

    def device_at(spot, which):
        spot = lax.rem(spot + 4 * chips, chips)
        side = lax.div(spot, half)
        depth = spot + side * (2 * half - 1 - 2 * spot)
        return (depth * 2 + side) * 2 + which

    partner = device_at(place, 1 - core)
    following = device_at(place + step, core)
    rows, hidden = inputs_ref.shape
    width = out_ref.shape[1]
    rank = shrink_ref.shape[0]
    resident_rows = cache_shrink_ref.shape[0]
    tile_rows = flat_shrink.shape[0]
    tiles = tile_rows // rank
    resident = resident_rows // rank
    new = tiles - resident
    slots = store_shrink_ref.shape[0]
    owners = [lax.div(tiles_ref[resident + t], slots) for t in range(new)]
    store_copies = [
        pltpu.make_async_copy(store_shrink_ref, store_shrink_buf, store_sem.at[0]),
        pltpu.make_async_copy(store_expand_ref, store_expand_buf, store_sem.at[1]),
    ]
    for copy in store_copies:
        copy.start()

    def weight_copy(slot):
        turn = lax.div(slot, 2)
        own = lax.rem(slot, 2)
        spot = place + (1 - 2 * own) * step * (1 + turn)
        which = own * core + (1 - own) * (1 - core)
        block = device_at(spot, which)
        column = pl.multiple_of(block * width, width)
        return pltpu.make_async_copy(
            weight_ref.at[:, pl.ds(column, width)], weight_buf.at[slot], weight_sem.at[slot]
        )

    def start_weight(slot, carry):
        weight_copy(slot).start()
        return carry

    lax.fori_loop(0, n, start_weight, 0)

    barrier = pltpu.get_barrier_semaphore()

    def greet(offset, carry):
        pl.semaphore_signal(
            barrier,
            inc=1,
            device_id={"tensor": lax.rem(me + offset, n)},
            device_id_type=MESH,
        )
        return carry

    lax.fori_loop(1, n, greet, 0)

    chosen = jnp.int32(0)
    for t in range(new):
        chosen += jnp.where(owners[t] == me, lax.rem(tiles_ref[resident + t], slots), 0)
    stored = store_magnitude_ref[...].astype(jnp.float32)
    stored = jnp.sum(
        jnp.where(lax.broadcasted_iota(jnp.int32, stored.shape, 0) == chosen, stored, 0.0),
        axis=0,
        keepdims=True,
    )
    for target in range(n):
        magnitude_ref[target] = stored[:, target * width : (target + 1) * width]
    for t in range(tiles):
        same = (row_adapter_ref[...] == tiles_ref[t]).astype(jnp.float32)
        row_mask_ref[pl.ds(t * rank, rank), :] = jnp.broadcast_to(same, (rank, rows))
    for copy in store_copies:
        copy.wait()
    shrink_ref[...] = store_shrink_buf[chosen]
    expand_ref[...] = store_expand_buf[chosen]
    pl.semaphore_wait(barrier, n - 1)

    def piece_parts(target):
        shrink_column = pl.multiple_of(target * hidden, 128)
        expand_column = pl.multiple_of(target * width, 128)
        return (
            (shrink_ref.at[:, pl.ds(shrink_column, hidden)], got_shrink),
            (expand_ref.at[:, pl.ds(expand_column, width)], got_expand),
            (magnitude_ref.at[target], got_magnitude),
        )

    def piece_copies(offset):
        target = lax.rem(me + offset, n)
        return [
            pltpu.make_async_remote_copy(
                src_ref=source,
                dst_ref=landing.at[me],
                send_sem=piece_send.at[kind, offset],
                recv_sem=piece_recv.at[kind, me],
                device_id={"tensor": target},
                device_id_type=MESH,
            )
            for kind, (source, landing) in enumerate(piece_parts(target))
        ]

    def start_pieces(offset, carry):
        for copy in piece_copies(offset):
            copy.start()
        return carry

    def piece_sent(offset, carry):
        for copy in piece_copies(offset):
            copy.wait_send()
        return carry

    def own_pieces():
        return [
            pltpu.make_async_copy(source, landing.at[me], piece_recv.at[kind, me])
            for kind, (source, landing) in enumerate(piece_parts(me))
        ]

    def piece_arrived(sender, carry):
        for kind, landing in enumerate((got_shrink, got_expand, got_magnitude)):
            pltpu.make_async_copy(
                landing.at[sender], landing.at[sender], piece_recv.at[kind, sender]
            ).wait()
        return carry

    def pair_copy(chain, turn):
        source, landing = ((base_pair_out, base_pair_in), (cross_pair_out, cross_pair_in))[chain]
        return pltpu.make_async_remote_copy(
            src_ref=source.at[turn],
            dst_ref=landing.at[turn],
            send_sem=pair_send.at[chain, turn],
            recv_sem=pair_recv.at[chain, turn],
            device_id={"tensor": partner},
            device_id_type=MESH,
        )

    def part_rows(chain, part):
        height = tile_rows if chain else rows
        low, high = height * part // PARTS, height * (part + 1) // PARTS
        if chain == 0 and part == PARTS - 1:
            high = rows + 8
        return pl.ds(low, high - low)

    def ring_copy(chain, turn, part):
        source, landing = ((base_ring_out, base_ring_in), (cross_ring_out, cross_ring_in))[chain]
        span = part_rows(chain, part)
        return pltpu.make_async_remote_copy(
            src_ref=source.at[turn, span],
            dst_ref=landing.at[turn, span],
            send_sem=ring_send.at[chain, part, turn],
            recv_sem=ring_recv.at[chain, part, turn],
            device_id={"tensor": following},
            device_id_type=MESH,
        )

    def small_copy(offset):
        return pltpu.make_async_remote_copy(
            src_ref=small_out,
            dst_ref=small_in.at[me],
            send_sem=small_send.at[offset],
            recv_sem=small_recv.at[me],
            device_id={"tensor": lax.rem(me + offset, n)},
            device_id_type=MESH,
        )

    def squares(slot):
        chunk = 64

        def add(index, total):
            part = weight_buf[slot, pl.ds(pl.multiple_of(index * chunk, chunk), chunk), :]
            part = part.astype(jnp.float32)
            return total + jnp.sum((part * part).reshape(chunk // 8, 8, width), axis=0)

        return lax.fori_loop(0, hidden // chunk, add, jnp.zeros((8, width), jnp.float32))

    def product(chain, slot):
        left = (inputs_ref, flat_shrink)[chain]
        return jnp.dot(left[...], weight_buf[slot], preferred_element_type=jnp.float32)

    def to_partner(chain, turn):
        slot = 2 * turn
        out = (base_pair_out, cross_pair_out)[chain]
        if chain == 0:
            weight_copy(slot).wait()
            out[turn, pl.ds(rows, 8), :] = squares(slot)
        out[turn, pl.ds(0, rows if chain == 0 else tile_rows), :] = product(chain, slot)
        pair_copy(chain, turn).start()

    def prepare(chain, turn):
        slot = 2 * turn + 1
        total = (base_ring_out, cross_ring_out)[chain]
        pair_in = (base_pair_in, cross_pair_in)[chain]
        if chain == 0:
            weight_copy(slot).wait()
            own_squares = squares(slot)
        own = product(chain, slot)
        pair_copy(chain, turn).wait_recv()
        height = own.shape[0]
        total[turn, pl.ds(0, height), :] = own + pair_in[turn, pl.ds(0, height), :]
        if chain == 0:
            total[turn, pl.ds(rows, 8), :] = own_squares + pair_in[turn, pl.ds(rows, 8), :]

    def ring_turn(chain, turn):
        total = (base_ring_out, cross_ring_out)[chain]
        ring_in = (base_ring_in, cross_ring_in)[chain]
        for part in range(PARTS):
            span = part_rows(chain, part)

            @pl.when(turn > 0)
            def _():
                ring_copy(chain, turn - 1, part).wait_recv()
                total[turn, span, :] += ring_in[turn - 1, span, :]

            @pl.when(turn < chips - 1)
            def _():
                ring_copy(chain, turn, part).start()

    def adapters_ready():
        lax.fori_loop(0, n, piece_arrived, 0)
        flat_shrink[pl.ds(0, resident_rows), :] = cache_shrink_ref[...]
        flat_expand[pl.ds(0, resident_rows), :] = cache_expand_ref[...]
        for tile in range(new):
            owner = owners[tile]
            target = pl.ds(resident_rows + tile * rank, rank)
            flat_shrink[target, :] = got_shrink[owner]
            flat_expand[target, :] = got_expand[owner]
        shrink = flat_shrink[...]
        contract = (((1,), (1,)), ((), ()))
        low = lax.dot_general(
            shrink, inputs_ref[...], contract, preferred_element_type=jnp.float32
        )
        gram = lax.dot_general(shrink, shrink, contract, preferred_element_type=jnp.float32)
        low = jnp.sum((low * row_mask_ref[...]).reshape(tiles, rank, rows), axis=0)
        gram = jnp.where(tile_mask(), gram, 0.0)
        gram = jnp.sum(gram.reshape(tiles, rank, tile_rows), axis=0)
        small_out[pl.ds(0, rank), :] = low
        small_out[pl.ds(rank, rank), :] = gram

        def send(offset, carry):
            small_copy(offset).start()
            return carry

        lax.fori_loop(1, n, send, 0)

    def tile_mask():
        shape = (tile_rows, tile_rows)
        first = lax.broadcasted_iota(jnp.int32, shape, 0) // rank
        second = lax.broadcasted_iota(jnp.int32, shape, 1) // rank
        return first == second

    for copy in own_pieces():
        copy.start()
    lax.fori_loop(1, n, start_pieces, 0)
    to_partner(0, 0)
    to_partner(0, 1)
    prepare(0, 0)

    def turn_body(turn, carry):
        @pl.when(turn < chips)
        def _():
            ring_turn(0, turn)

        @pl.when(turn >= LAG)
        def _():
            ring_turn(1, turn - LAG)

        @pl.when(turn < chips - 2)
        def _():
            to_partner(0, turn + 2)

        @pl.when(turn < chips - 1)
        def _():
            prepare(0, turn + 1)

        @pl.when(turn == LAG - 1)
        def _():
            adapters_ready()
            to_partner(1, 0)

        @pl.when((turn >= LAG - 1) & (turn < chips + LAG - 2))
        def _():
            to_partner(1, turn - LAG + 2)

        @pl.when((turn >= LAG - 1) & (turn < chips + LAG - 1))
        def _():
            prepare(1, turn - LAG + 1)

        return carry

    lax.fori_loop(0, chips + LAG, turn_body, 0)

    def add_small(offset, total):
        sender = lax.rem(me + offset, n)
        pltpu.make_async_copy(
            small_in.at[sender], small_in.at[sender], small_recv.at[sender]
        ).wait()
        return total + small_in[sender]

    small = lax.fori_loop(1, n, add_small, small_out[...])
    low = jnp.concatenate([small[:rank]] * tiles, 0)
    gram = jnp.where(tile_mask(), jnp.concatenate([small[rank:]] * tiles, 0), 0.0)
    expand = flat_expand[...]
    wide = expand.astype(jnp.float32)
    quadratic = exact_dot(gram, expand, ((1,), (0,)))
    change = jnp.sum(
        (wide * (cross_ring_out[chips - 1] + quadratic)).reshape(tiles, rank, width), axis=1
    )
    column_squares = jnp.sum(base_ring_out[chips - 1, pl.ds(rows, 8), :], axis=0, keepdims=True)
    squared_norm = column_squares + 2.0 * ADAPTER_SCALING * change
    magnitude = jnp.concatenate(
        [cache_magnitude_ref[...].astype(jnp.float32)] + [got_magnitude[owners[t]] for t in range(new)], 0
    )
    factor = magnitude / jnp.sqrt(squared_norm)
    row_mask = row_mask_ref[...]
    update = exact_dot(low * row_mask, expand, ((0,), (0,)))
    spread = jnp.broadcast_to(factor[:, None, :], (tiles, rank, width)).reshape(tile_rows, width)
    pick = lax.broadcasted_iota(jnp.int32, row_mask.shape, 0) % rank == 0
    pick = jnp.where(pick, row_mask, 0.0).astype(jnp.bfloat16)
    multiplier = sum(
        lax.dot_general(
            pick, part, (((0,), (0,)), ((), ())), preferred_element_type=jnp.float32
        )
        for part in reversed(split3(spread))
    )
    base = base_ring_out[chips - 1, pl.ds(0, rows), :]
    out_ref[...] = (multiplier * (base + ADAPTER_SCALING * update)).astype(out_ref.dtype)

    lax.fori_loop(1, n, piece_sent, 0)

    def small_sent(offset, carry):
        small_copy(offset).wait_send()
        return carry

    lax.fori_loop(1, n, small_sent, 0)

    def turn_sent(turn, carry):
        for chain in range(2):
            pair_copy(chain, turn).wait_send()

            @pl.when(turn < chips - 1)
            def _():
                for part in range(PARTS):
                    ring_copy(chain, turn, part).wait_send()

        return carry

    lax.fori_loop(0, chips, turn_sent, 0)


def fused_local(
    n,
    inputs,
    base_weight,
    cache_shrink,
    cache_expand,
    cache_magnitude,
    store_shrink,
    store_expand,
    store_magnitude,
    tile_adapter,
    row_adapter,
):
    slot_count, rank, all_hidden = store_shrink.shape
    all_width = store_expand.shape[2]
    resident, _, hidden = cache_shrink.shape
    width = cache_expand.shape[2]
    rows = inputs.shape[0]
    tiles = tile_adapter.shape[0]
    tile_rows = tiles * rank
    chips = n // 2
    tall = rows + 8
    vmem = pl.BlockSpec(memory_space=pltpu.VMEM)
    hbm = pl.BlockSpec(memory_space=pl.ANY)
    return pl.pallas_call(
        functools.partial(fused_kernel, n),
        out_shape=jax.ShapeDtypeStruct((rows, width), jnp.bfloat16),
        in_specs=[pl.BlockSpec(memory_space=pltpu.SMEM), vmem, hbm]
        + [vmem] * 3
        + [hbm] * 2
        + [vmem] * 2,
        out_specs=vmem,
        scratch_shapes=[
            pltpu.VMEM((n, hidden, width), jnp.bfloat16),
            pltpu.VMEM((slot_count, rank, all_hidden), jnp.bfloat16),
            pltpu.VMEM((slot_count, rank, all_width), jnp.bfloat16),
            pltpu.VMEM((rank, all_hidden), jnp.bfloat16),
            pltpu.VMEM((rank, all_width), jnp.bfloat16),
            pltpu.VMEM((n, 1, width), jnp.float32),
            pltpu.VMEM((tile_rows, rows), jnp.float32),
            pltpu.VMEM((n, rank, hidden), jnp.bfloat16),
            pltpu.VMEM((n, rank, width), jnp.bfloat16),
            pltpu.VMEM((n, 1, width), jnp.float32),
            pltpu.VMEM((tile_rows, hidden), jnp.bfloat16),
            pltpu.VMEM((tile_rows, width), jnp.bfloat16),
            pltpu.VMEM((chips, tall, width), jnp.float32),
            pltpu.VMEM((chips, tall, width), jnp.float32),
            pltpu.VMEM((chips, tall, width), jnp.float32),
            pltpu.VMEM((chips - 1, tall, width), jnp.float32),
            pltpu.VMEM((chips, tile_rows, width), jnp.float32),
            pltpu.VMEM((chips, tile_rows, width), jnp.float32),
            pltpu.VMEM((chips, tile_rows, width), jnp.float32),
            pltpu.VMEM((chips - 1, tile_rows, width), jnp.float32),
            pltpu.VMEM((2 * rank, rows), jnp.float32),
            pltpu.VMEM((n, 2 * rank, rows), jnp.float32),
            pltpu.SemaphoreType.DMA((n,)),
            pltpu.SemaphoreType.DMA((2,)),
            pltpu.SemaphoreType.DMA((3, n)),
            pltpu.SemaphoreType.DMA((3, n)),
            pltpu.SemaphoreType.DMA((2, chips)),
            pltpu.SemaphoreType.DMA((2, chips)),
            pltpu.SemaphoreType.DMA((2, PARTS, chips)),
            pltpu.SemaphoreType.DMA((2, PARTS, chips)),
            pltpu.SemaphoreType.DMA((n,)),
            pltpu.SemaphoreType.DMA((n,)),
        ],
        compiler_params=pltpu.CompilerParams(
            collective_id=0, has_side_effects=True, vmem_limit_bytes=56 * 1024 * 1024
        ),
    )(
        tile_adapter,
        inputs,
        base_weight,
        cache_shrink.reshape(resident * rank, hidden),
        cache_expand.reshape(resident * rank, width),
        cache_magnitude,
        store_shrink,
        store_expand,
        store_magnitude,
        row_adapter.reshape(1, rows),
    )


def fits_kernel(n, inputs, cache_shrink, cache_expand, tile_adapter):
    rank = cache_shrink.shape[1]
    rows = inputs.shape[0]
    tile_rows = tile_adapter.shape[0] * rank
    return (
        n % 4 == 0
        and cache_shrink.shape[2] % 128 == 0
        and cache_expand.shape[2] % 128 == 0
        and rank % 16 == 0
        and rows == tile_rows
        and rows % 128 == 0
        and n * cache_shrink.shape[2] * cache_expand.shape[2] <= 2**23
    )


def local(n, *args):
    if fits_kernel(n, args[0], args[2], args[3], args[8]):
        return fused_local(n, *args)
    return plain_local(*args)


def solution(mesh):
    in_specs = (
        P("groups", "tensor"),
        P("tensor", None),
        P("groups", None, "tensor"),
        P("groups", None, "tensor"),
        P("groups", "tensor"),
        P(("groups", "tensor"), None, None),
        P(("groups", "tensor"), None, None),
        P(("groups", "tensor"), None),
        P("groups"),
        P("groups"),
    )
    out_specs = P("groups", "tensor")
    body = functools.partial(local, mesh.shape["tensor"])
    return jax.shard_map(body, mesh=mesh, in_specs=in_specs, out_specs=out_specs, check_vma=False)
```

```python
import functools

import jax
import jax.numpy as jnp
from jax import lax
from jax.experimental import pallas as pl
from jax.experimental.pallas import tpu as pltpu
from jax.sharding import PartitionSpec as P

ADAPTER_SCALING = 2.0


def plain_local(
    inputs,
    base_weight,
    cache_shrink,
    cache_expand,
    cache_magnitude,
    store_shrink,
    store_expand,
    store_magnitude,
    tile_adapter,
    row_adapter,
):
    highest_precision = lax.Precision.HIGHEST
    position = lax.axis_index("tensor")
    slot_count = store_shrink.shape[0]
    resident = cache_shrink.shape[0]
    new_ids = tile_adapter[resident:]
    owners = new_ids // slot_count
    owned = owners == position
    chosen = jnp.sum(jnp.where(owned, new_ids % slot_count, 0))
    present = jnp.any(owned)

    def select_piece(stored):
        segment = lax.dynamic_index_in_dim(stored, chosen, 0, keepdims=True)
        return jnp.where(present, segment, jnp.zeros_like(segment))

    sent_shrink = select_piece(store_shrink)
    sent_expand = select_piece(store_expand)
    sent_magnitude = select_piece(store_magnitude)[:, None, :]
    got_shrink, got_expand, got_magnitude = (
        lax.all_to_all(sent_shrink, "tensor", split_axis=2, concat_axis=0, tiled=True),
        lax.all_to_all(sent_expand, "tensor", split_axis=2, concat_axis=0, tiled=True),
        lax.all_to_all(sent_magnitude, "tensor", split_axis=2, concat_axis=0, tiled=True),
    )
    down_factor = jnp.concatenate([cache_shrink, jnp.take(got_shrink, owners, axis=0)], 0)
    expand = jnp.concatenate([cache_expand, jnp.take(got_expand, owners, axis=0)], 0)
    magnitude = jnp.concatenate(
        [cache_magnitude, jnp.take(got_magnitude, owners, axis=0)[:, 0, :]], 0
    ).astype(jnp.float32)
    tile_count = down_factor.shape[0]
    rank_size = down_factor.shape[1]
    row_count = inputs.shape[0]
    own_width = expand.shape[2]
    flat_shrink = down_factor.reshape(tile_count * rank_size, down_factor.shape[2])
    row_tile = (row_adapter[:, None] == tile_adapter[None, :]).astype(jnp.float32)
    projected = lax.dot_general(
        inputs, flat_shrink, (((1,), (1,)), ((), ())), preferred_element_type=jnp.float32
    )
    low_part = jnp.sum(
        row_tile[:, :, None] * projected.reshape(row_count, tile_count, rank_size), axis=1
    )
    base_part = jnp.dot(inputs, base_weight, preferred_element_type=jnp.float32)
    expand_wide = expand.astype(jnp.float32)
    col_part = jnp.sum(jnp.square(base_weight.astype(jnp.float32)), axis=0)
    partial_gram_matrix = jnp.einsum(
        "aig,ahg->aih", down_factor, down_factor, preferred_element_type=jnp.float32
    )
    low, gram_sum, column_square_sums = lax.psum(
        (low_part, partial_gram_matrix, col_part), "tensor"
    )
    cross = lax.psum_scatter(
        lax.dot_general(
            base_weight, flat_shrink, (((0,), (1,)), ((), ())), preferred_element_type=jnp.float32
        ),
        "tensor",
        scatter_dimension=0,
        tiled=True,
    ).reshape(own_width, tile_count, rank_size)
    frozen_output = lax.psum_scatter(base_part, "tensor", scatter_dimension=1, tiled=True)
    local_column_slice = lax.dynamic_slice_in_dim(
        column_square_sums, position * own_width, own_width
    )
    linear_term = jnp.einsum("dtr,trd->td", cross, expand_wide, precision=highest_precision)
    quadratic_term = jnp.sum(
        expand_wide
        * jnp.einsum("trq,tqd->trd", gram_sum, expand_wide, precision=highest_precision),
        axis=1,
    )
    squared_norm = (
        local_column_slice[None, :]
        + 2.0 * ADAPTER_SCALING * linear_term
        + ADAPTER_SCALING * ADAPTER_SCALING * quadratic_term
    )
    factor = magnitude / jnp.sqrt(squared_norm)
    spread = (row_tile[:, :, None] * low[:, None, :]).reshape(row_count, tile_count * rank_size)
    low_rank_update = jnp.dot(
        spread, expand_wide.reshape(tile_count * rank_size, own_width), precision=highest_precision
    )
    row_multiplier = jnp.dot(row_tile, factor, precision=highest_precision)
    return (row_multiplier * (frozen_output + ADAPTER_SCALING * low_rank_update)).astype(
        jnp.bfloat16
    )


LAG = 1
PARTS = 4
MESH = pl.DeviceIdType.MESH


def split3(value):
    high = value.astype(jnp.bfloat16)
    rest = value - high.astype(jnp.float32)
    middle = rest.astype(jnp.bfloat16)
    low = (rest - middle.astype(jnp.float32)).astype(jnp.bfloat16)
    return high, middle, low


def exact_dot(left, right, dims):
    return sum(
        lax.dot_general(part, right, (dims, ((), ())), preferred_element_type=jnp.float32)
        for part in reversed(split3(left))
    )


def fused_kernel(
    n,
    tiles_ref,
    inputs_ref,
    weight_ref,
    cache_shrink_ref,
    cache_expand_ref,
    cache_magnitude_ref,
    store_shrink_ref,
    store_expand_ref,
    store_magnitude_ref,
    row_adapter_ref,
    out_ref,
    weight_buf,
    store_shrink_buf,
    store_expand_buf,
    shrink_ref,
    expand_ref,
    magnitude_ref,
    row_mask_ref,
    got_shrink,
    got_expand,
    got_magnitude,
    flat_shrink,
    flat_expand,
    base_pair_out,
    base_pair_in,
    base_ring_out,
    base_ring_in,
    cross_pair_out,
    cross_pair_in,
    cross_ring_out,
    cross_ring_in,
    small_out,
    small_in,
    weight_sem,
    store_sem,
    piece_send,
    piece_recv,
    pair_send,
    pair_recv,
    ring_send,
    ring_recv,
    small_send,
    small_recv,
):
    me = lax.axis_index("tensor")
    chips = n // 2
    half = n // 4
    core = lax.rem(me, 2)
    chip = lax.div(me, 2)
    across = lax.rem(chip, 2)
    along = lax.div(chip, 2)
    place = along + across * (2 * half - 1 - 2 * along)
    step = 1 - 2 * core

    def device_at(spot, which):
        spot = lax.rem(spot + 4 * chips, chips)
        side = lax.div(spot, half)
        depth = spot + side * (2 * half - 1 - 2 * spot)
        return (depth * 2 + side) * 2 + which

    partner = device_at(place, 1 - core)
    following = device_at(place + step, core)
    rows, hidden = inputs_ref.shape
    width = out_ref.shape[1]
    rank = shrink_ref.shape[0]
    resident_rows = cache_shrink_ref.shape[0]
    tile_rows = flat_shrink.shape[0]
    tiles = tile_rows // rank
    resident = resident_rows // rank
    new = tiles - resident
    slots = store_shrink_ref.shape[0]
    owners = [lax.div(tiles_ref[resident + t], slots) for t in range(new)]
    store_copies = [
        pltpu.make_async_copy(store_shrink_ref, store_shrink_buf, store_sem.at[0]),
        pltpu.make_async_copy(store_expand_ref, store_expand_buf, store_sem.at[1]),
    ]
    for copy in store_copies:
        copy.start()

    def weight_copy(slot):
        turn = lax.div(slot, 2)
        own = lax.rem(slot, 2)
        spot = place + (1 - 2 * own) * step * (1 + turn)
        which = own * core + (1 - own) * (1 - core)
        block = device_at(spot, which)
        column = pl.multiple_of(block * width, width)
        return pltpu.make_async_copy(
            weight_ref.at[:, pl.ds(column, width)], weight_buf.at[slot], weight_sem.at[slot]
        )

    def start_weight(slot, carry):
        weight_copy(slot).start()
        return carry

    lax.fori_loop(0, n, start_weight, 0)

    barrier = pltpu.get_barrier_semaphore()

    def greet(offset, carry):
        pl.semaphore_signal(
            barrier,
            inc=1,
            device_id={"tensor": lax.rem(me + offset, n)},
            device_id_type=MESH,
        )
        return carry

    lax.fori_loop(1, n, greet, 0)

    chosen = jnp.int32(0)
    for t in range(new):
        chosen += jnp.where(owners[t] == me, lax.rem(tiles_ref[resident + t], slots), 0)
    stored = store_magnitude_ref[...].astype(jnp.float32)
    stored = jnp.sum(
        jnp.where(lax.broadcasted_iota(jnp.int32, stored.shape, 0) == chosen, stored, 0.0),
        axis=0,
        keepdims=True,
    )
    for target in range(n):
        magnitude_ref[target] = stored[:, target * width : (target + 1) * width]
    for t in range(tiles):
        same = (row_adapter_ref[...] == tiles_ref[t]).astype(jnp.float32)
        row_mask_ref[pl.ds(t * rank, rank), :] = jnp.broadcast_to(same, (rank, rows))
    for copy in store_copies:
        copy.wait()
    shrink_ref[...] = store_shrink_buf[chosen]
    expand_ref[...] = store_expand_buf[chosen]
    pl.semaphore_wait(barrier, n - 1)

    def piece_parts(target):
        shrink_column = pl.multiple_of(target * hidden, 128)
        expand_column = pl.multiple_of(target * width, 128)
        return (
            (shrink_ref.at[:, pl.ds(shrink_column, hidden)], got_shrink),
            (expand_ref.at[:, pl.ds(expand_column, width)], got_expand),
            (magnitude_ref.at[target], got_magnitude),
        )

    def piece_copies(offset, kinds=(0, 1, 2)):
        target = lax.rem(me + offset, n)
        return [
            pltpu.make_async_remote_copy(
                src_ref=source,
                dst_ref=landing.at[me],
                send_sem=piece_send.at[kind, offset],
                recv_sem=piece_recv.at[kind, me],
                device_id={"tensor": target},
                device_id_type=MESH,
            )
            for kind, (source, landing) in enumerate(piece_parts(target))
            if kind in kinds
        ]

    def start_shrink(offset, carry):
        for copy in piece_copies(offset, (0,)):
            copy.start()
        return carry

    def start_others(offset, carry):
        for copy in piece_copies(offset, (1, 2)):
            copy.start()
        return carry

    def piece_sent(offset, carry):
        for copy in piece_copies(offset):
            copy.wait_send()
        return carry

    def own_pieces():
        return [
            pltpu.make_async_copy(source, landing.at[me], piece_recv.at[kind, me])
            for kind, (source, landing) in enumerate(piece_parts(me))
        ]

    def landed(kind, sender):
        landing = (got_shrink, got_expand, got_magnitude)[kind]
        pltpu.make_async_copy(
            landing.at[sender], landing.at[sender], piece_recv.at[kind, sender]
        ).wait()

    def shrink_arrived(sender, carry):
        landed(0, sender)
        return carry

    def others_arrived(sender, carry):
        landed(1, sender)
        landed(2, sender)
        return carry

    def pair_copy(chain, turn):
        source, landing = ((base_pair_out, base_pair_in), (cross_pair_out, cross_pair_in))[chain]
        return pltpu.make_async_remote_copy(
            src_ref=source.at[turn],
            dst_ref=landing.at[turn],
            send_sem=pair_send.at[chain, turn],
            recv_sem=pair_recv.at[chain, turn],
            device_id={"tensor": partner},
            device_id_type=MESH,
        )

    def part_rows(chain, part):
        height = tile_rows if chain else rows
        low, high = height * part // PARTS, height * (part + 1) // PARTS
        if chain == 0 and part == PARTS - 1:
            high = rows + 8
        return pl.ds(low, high - low)

    def ring_copy(chain, turn, part):
        source, landing = ((base_ring_out, base_ring_in), (cross_ring_out, cross_ring_in))[chain]
        span = part_rows(chain, part)
        return pltpu.make_async_remote_copy(
            src_ref=source.at[turn, span],
            dst_ref=landing.at[turn, span],
            send_sem=ring_send.at[chain, part, turn],
            recv_sem=ring_recv.at[chain, part, turn],
            device_id={"tensor": following},
            device_id_type=MESH,
        )

    def small_copy(offset):
        return pltpu.make_async_remote_copy(
            src_ref=small_out,
            dst_ref=small_in.at[me],
            send_sem=small_send.at[offset],
            recv_sem=small_recv.at[me],
            device_id={"tensor": lax.rem(me + offset, n)},
            device_id_type=MESH,
        )

    def squares(slot):
        chunk = 64

        def add(index, total):
            part = weight_buf[slot, pl.ds(pl.multiple_of(index * chunk, chunk), chunk), :]
            part = part.astype(jnp.float32)
            return total + jnp.sum((part * part).reshape(chunk // 8, 8, width), axis=0)

        return lax.fori_loop(0, hidden // chunk, add, jnp.zeros((8, width), jnp.float32))

    def product(chain, slot):
        left = (inputs_ref, flat_shrink)[chain]
        return jnp.dot(left[...], weight_buf[slot], preferred_element_type=jnp.float32)

    def to_partner(chain, turn):
        slot = 2 * turn
        out = (base_pair_out, cross_pair_out)[chain]
        if chain == 0:
            weight_copy(slot).wait()
            out[turn, pl.ds(rows, 8), :] = squares(slot)
        out[turn, pl.ds(0, rows if chain == 0 else tile_rows), :] = product(chain, slot)
        pair_copy(chain, turn).start()

    def prepare(chain, turn):
        slot = 2 * turn + 1
        total = (base_ring_out, cross_ring_out)[chain]
        pair_in = (base_pair_in, cross_pair_in)[chain]
        if chain == 0:
            weight_copy(slot).wait()
            own_squares = squares(slot)
        own = product(chain, slot)
        pair_copy(chain, turn).wait_recv()
        height = own.shape[0]
        total[turn, pl.ds(0, height), :] = own + pair_in[turn, pl.ds(0, height), :]
        if chain == 0:
            total[turn, pl.ds(rows, 8), :] = own_squares + pair_in[turn, pl.ds(rows, 8), :]

    def ring_turn(chain, turn):
        total = (base_ring_out, cross_ring_out)[chain]
        ring_in = (base_ring_in, cross_ring_in)[chain]
        for part in range(PARTS):
            span = part_rows(chain, part)

            @pl.when(turn > 0)
            def _():
                ring_copy(chain, turn - 1, part).wait_recv()
                total[turn, span, :] += ring_in[turn - 1, span, :]

            @pl.when(turn < chips - 1)
            def _():
                ring_copy(chain, turn, part).start()

    def adapters_ready():
        lax.fori_loop(0, n, shrink_arrived, 0)
        flat_shrink[pl.ds(0, resident_rows), :] = cache_shrink_ref[...]
        for tile in range(new):
            owner = owners[tile]
            target = pl.ds(resident_rows + tile * rank, rank)
            flat_shrink[target, :] = got_shrink[owner]
        shrink = flat_shrink[...]
        contract = (((1,), (1,)), ((), ()))
        low = lax.dot_general(
            shrink, inputs_ref[...], contract, preferred_element_type=jnp.float32
        )
        gram = lax.dot_general(shrink, shrink, contract, preferred_element_type=jnp.float32)
        low = jnp.sum((low * row_mask_ref[...]).reshape(tiles, rank, rows), axis=0)
        gram = jnp.where(tile_mask(), gram, 0.0)
        gram = jnp.sum(gram.reshape(tiles, rank, tile_rows), axis=0)
        small_out[pl.ds(0, rank), :] = low
        small_out[pl.ds(rank, rank), :] = gram

        def send(offset, carry):
            small_copy(offset).start()
            return carry

        lax.fori_loop(1, n, send, 0)
        lax.fori_loop(1, n, start_others, 0)

    def tile_mask():
        shape = (tile_rows, tile_rows)
        first = lax.broadcasted_iota(jnp.int32, shape, 0) // rank
        second = lax.broadcasted_iota(jnp.int32, shape, 1) // rank
        return first == second

    for copy in own_pieces():
        copy.start()
    lax.fori_loop(1, n, start_shrink, 0)
    to_partner(0, 0)
    to_partner(0, 1)
    prepare(0, 0)

    def turn_body(turn, carry):
        @pl.when(turn < chips)
        def _():
            ring_turn(0, turn)

        @pl.when(turn >= LAG)
        def _():
            ring_turn(1, turn - LAG)

        @pl.when(turn < chips - 2)
        def _():
            to_partner(0, turn + 2)

        @pl.when(turn < chips - 1)
        def _():
            prepare(0, turn + 1)

        @pl.when(turn == LAG - 1)
        def _():
            adapters_ready()
            to_partner(1, 0)

        @pl.when((turn >= LAG - 1) & (turn < chips + LAG - 2))
        def _():
            to_partner(1, turn - LAG + 2)

        @pl.when((turn >= LAG - 1) & (turn < chips + LAG - 1))
        def _():
            prepare(1, turn - LAG + 1)

        return carry

    lax.fori_loop(0, chips + LAG, turn_body, 0)

    def add_small(offset, total):
        sender = lax.rem(me + offset, n)
        pltpu.make_async_copy(
            small_in.at[sender], small_in.at[sender], small_recv.at[sender]
        ).wait()
        return total + small_in[sender]

    small = lax.fori_loop(1, n, add_small, small_out[...])
    low = jnp.concatenate([small[:rank]] * tiles, 0)
    gram = jnp.where(tile_mask(), jnp.concatenate([small[rank:]] * tiles, 0), 0.0)
    lax.fori_loop(0, n, others_arrived, 0)
    flat_expand[pl.ds(0, resident_rows), :] = cache_expand_ref[...]
    for tile in range(new):
        flat_expand[pl.ds(resident_rows + tile * rank, rank), :] = got_expand[owners[tile]]
    expand = flat_expand[...]
    wide = expand.astype(jnp.float32)
    quadratic = exact_dot(gram, expand, ((1,), (0,)))
    change = jnp.sum(
        (wide * (cross_ring_out[chips - 1] + quadratic)).reshape(tiles, rank, width), axis=1
    )
    column_squares = jnp.sum(base_ring_out[chips - 1, pl.ds(rows, 8), :], axis=0, keepdims=True)
    squared_norm = column_squares + 2.0 * ADAPTER_SCALING * change
    magnitude = jnp.concatenate(
        [cache_magnitude_ref[...].astype(jnp.float32)] + [got_magnitude[owners[t]] for t in range(new)], 0
    )
    factor = magnitude / jnp.sqrt(squared_norm)
    row_mask = row_mask_ref[...]
    update = exact_dot(low * row_mask, expand, ((0,), (0,)))
    spread = jnp.broadcast_to(factor[:, None, :], (tiles, rank, width)).reshape(tile_rows, width)
    pick = lax.broadcasted_iota(jnp.int32, row_mask.shape, 0) % rank == 0
    pick = jnp.where(pick, row_mask, 0.0).astype(jnp.bfloat16)
    multiplier = sum(
        lax.dot_general(
            pick, part, (((0,), (0,)), ((), ())), preferred_element_type=jnp.float32
        )
        for part in reversed(split3(spread))
    )
    base = base_ring_out[chips - 1, pl.ds(0, rows), :]
    out_ref[...] = (multiplier * (base + ADAPTER_SCALING * update)).astype(out_ref.dtype)

    lax.fori_loop(1, n, piece_sent, 0)

    def small_sent(offset, carry):
        small_copy(offset).wait_send()
        return carry

    lax.fori_loop(1, n, small_sent, 0)

    def turn_sent(turn, carry):
        for chain in range(2):
            pair_copy(chain, turn).wait_send()

            @pl.when(turn < chips - 1)
            def _():
                for part in range(PARTS):
                    ring_copy(chain, turn, part).wait_send()

        return carry

    lax.fori_loop(0, chips, turn_sent, 0)


def fused_local(
    n,
    inputs,
    base_weight,
    cache_shrink,
    cache_expand,
    cache_magnitude,
    store_shrink,
    store_expand,
    store_magnitude,
    tile_adapter,
    row_adapter,
):
    slot_count, rank, all_hidden = store_shrink.shape
    all_width = store_expand.shape[2]
    resident, _, hidden = cache_shrink.shape
    width = cache_expand.shape[2]
    rows = inputs.shape[0]
    tiles = tile_adapter.shape[0]
    tile_rows = tiles * rank
    chips = n // 2
    tall = rows + 8
    vmem = pl.BlockSpec(memory_space=pltpu.VMEM)
    hbm = pl.BlockSpec(memory_space=pl.ANY)
    return pl.pallas_call(
        functools.partial(fused_kernel, n),
        out_shape=jax.ShapeDtypeStruct((rows, width), jnp.bfloat16),
        in_specs=[pl.BlockSpec(memory_space=pltpu.SMEM), vmem, hbm]
        + [vmem] * 3
        + [hbm] * 2
        + [vmem] * 2,
        out_specs=vmem,
        scratch_shapes=[
            pltpu.VMEM((n, hidden, width), jnp.bfloat16),
            pltpu.VMEM((slot_count, rank, all_hidden), jnp.bfloat16),
            pltpu.VMEM((slot_count, rank, all_width), jnp.bfloat16),
            pltpu.VMEM((rank, all_hidden), jnp.bfloat16),
            pltpu.VMEM((rank, all_width), jnp.bfloat16),
            pltpu.VMEM((n, 1, width), jnp.float32),
            pltpu.VMEM((tile_rows, rows), jnp.float32),
            pltpu.VMEM((n, rank, hidden), jnp.bfloat16),
            pltpu.VMEM((n, rank, width), jnp.bfloat16),
            pltpu.VMEM((n, 1, width), jnp.float32),
            pltpu.VMEM((tile_rows, hidden), jnp.bfloat16),
            pltpu.VMEM((tile_rows, width), jnp.bfloat16),
            pltpu.VMEM((chips, tall, width), jnp.float32),
            pltpu.VMEM((chips, tall, width), jnp.float32),
            pltpu.VMEM((chips, tall, width), jnp.float32),
            pltpu.VMEM((chips - 1, tall, width), jnp.float32),
            pltpu.VMEM((chips, tile_rows, width), jnp.float32),
            pltpu.VMEM((chips, tile_rows, width), jnp.float32),
            pltpu.VMEM((chips, tile_rows, width), jnp.float32),
            pltpu.VMEM((chips - 1, tile_rows, width), jnp.float32),
            pltpu.VMEM((2 * rank, rows), jnp.float32),
            pltpu.VMEM((n, 2 * rank, rows), jnp.float32),
            pltpu.SemaphoreType.DMA((n,)),
            pltpu.SemaphoreType.DMA((2,)),
            pltpu.SemaphoreType.DMA((3, n)),
            pltpu.SemaphoreType.DMA((3, n)),
            pltpu.SemaphoreType.DMA((2, chips)),
            pltpu.SemaphoreType.DMA((2, chips)),
            pltpu.SemaphoreType.DMA((2, PARTS, chips)),
            pltpu.SemaphoreType.DMA((2, PARTS, chips)),
            pltpu.SemaphoreType.DMA((n,)),
            pltpu.SemaphoreType.DMA((n,)),
        ],
        compiler_params=pltpu.CompilerParams(
            collective_id=0, has_side_effects=True, vmem_limit_bytes=56 * 1024 * 1024
        ),
    )(
        tile_adapter,
        inputs,
        base_weight,
        cache_shrink.reshape(resident * rank, hidden),
        cache_expand.reshape(resident * rank, width),
        cache_magnitude,
        store_shrink,
        store_expand,
        store_magnitude,
        row_adapter.reshape(1, rows),
    )


def fits_kernel(n, inputs, cache_shrink, cache_expand, tile_adapter):
    rank = cache_shrink.shape[1]
    rows = inputs.shape[0]
    tile_rows = tile_adapter.shape[0] * rank
    return (
        n % 4 == 0
        and cache_shrink.shape[2] % 128 == 0
        and cache_expand.shape[2] % 128 == 0
        and rank % 16 == 0
        and rows == tile_rows
        and rows % 128 == 0
        and n * cache_shrink.shape[2] * cache_expand.shape[2] <= 2**23
    )


def local(n, *args):
    if fits_kernel(n, args[0], args[2], args[3], args[8]):
        return fused_local(n, *args)
    return plain_local(*args)


def solution(mesh):
    in_specs = (
        P("groups", "tensor"),
        P("tensor", None),
        P("groups", None, "tensor"),
        P("groups", None, "tensor"),
        P("groups", "tensor"),
        P(("groups", "tensor"), None, None),
        P(("groups", "tensor"), None, None),
        P(("groups", "tensor"), None),
        P("groups"),
        P("groups"),
    )
    out_specs = P("groups", "tensor")
    body = functools.partial(local, mesh.shape["tensor"])
    return jax.shard_map(body, mesh=mesh, in_specs=in_specs, out_specs=out_specs, check_vma=False)
```
